32 devices in a mesh: outer: 2 (over y), inner: 4 (over z), head: 4 (over x, core).
Axes of the slice: x: 2, y: 2, z: 4, core: 2. Of those that a mesh axis runs over, the one named last changes fastest.
Arguments:
- queries: bfloat16 [8192, 4096], P(('outer', 'inner'), 'head'), may hold values from -6 to 6
- keys: bfloat16 [8192, 4096], P(('outer', 'inner'), 'head'), may hold values from -0.046875 to 0.046875
- values: bfloat16 [8192, 4096], P(('outer', 'inner'), 'head'), may hold values from -36 to 36
- out_grad: bfloat16 [8192, 4096], P(('outer', 'inner'), 'head'), may hold values from -6 to 6
- log_key_decay: float32 [8192, 4096], P(('outer', 'inner'), 'head'), may hold values from -0.62 to 0
- value_rate: float32 [4096], P('head'), may hold values from 1.2207031e-05 to 0.05
- norm_gain: float32 [4096], P('head'), may hold values from 0.1 to 1.9
Outputs:
- query_grad: bfloat16 [8192, 4096], P(('outer', 'inner'), 'head')
- key_grad: bfloat16 [8192, 4096], P(('outer', 'inner'), 'head')
- value_grad: bfloat16 [8192, 4096], P(('outer', 'inner'), 'head')
- gain_grad: float32 [4096], P('head')
The draws below stay inside these ranges and needn't reach their ends.
All inputs are finite; a program needn't handle non-finite values.
Results may differ from the reference program's by a relative error of at most 0.001.
Values sent between devices are 32-bit elements; how exact they have to be, the bound alone decides.
A program may use at most 192 MiB of HBM per device.

```python
import math
import jax
import jax.numpy as jnp
from jax import lax

HEADS = 32
DK = 128
DV = 128
BL = 128
T_DEV = 1024
TOKENS = 8192


def draw_log_key_decay(key, part):
    columns = HEADS * DK
    every_key_row = jax.random.split(key, 7)
    fast_rate = jnp.exp(jax.random.uniform(every_key_row[0], (columns,), jnp.float32, math.log(1.0 / 50.0), math.log(1.0 / 30.0)))
    slow_rate = jnp.exp(jax.random.uniform(every_key_row[1], (columns,), jnp.float32, math.log(0.1 / TOKENS), math.log(1.0 / TOKENS)))
    fast_share = 0.5
    chooser = jax.random.uniform(every_key_row[2], (columns,), jnp.float32)
    decay_rate = jnp.where(chooser < fast_share, fast_rate, slow_rate)
    segments = TOKENS // T_DEV
    segment_factor = jnp.exp(jax.random.uniform(every_key_row[3], (segments, 1, columns), jnp.float32, math.log(0.5), math.log(2.0)))
    jitter = jax.random.uniform(every_key_row[4], (segments, T_DEV, columns), jnp.float32, 0.5, 1.5)
    baseline_decay = -(decay_rate[None, None, :] * jitter * segment_factor).reshape(TOKENS, columns)
    permuted_order = jax.random.permutation(every_key_row[5], TOKENS)
    spike_depth = jax.random.uniform(every_key_row[6], (2,), jnp.float32, 0.22, 0.51)
    token_positions = jnp.arange(TOKENS)
    spike_loss = jnp.where(token_positions == permuted_order[0], -spike_depth[0], 0.0) + jnp.where(token_positions == permuted_order[1], -spike_depth[1], 0.0)
    return baseline_decay + spike_loss[:, None]


def draw_values(key, part):
    columns = HEADS * DV
    every_key_row = jax.random.split(key, 4)
    current_head_index = (jnp.arange(columns) // DV).astype(jnp.float32)
    head_scale = 3.0 ** (current_head_index / (HEADS - 1))
    channel_scale = jnp.exp(jax.random.uniform(every_key_row[0], (columns,), jnp.float32, math.log(0.3), math.log(3.0)))
    per_token_scale = jnp.exp(jax.random.uniform(every_key_row[1], (TOKENS, 1), jnp.float32, math.log(0.5), math.log(2.0)))
    noise = jnp.clip(jax.random.normal(every_key_row[3], (TOKENS, columns), jnp.float32), -4.0, 4.0)
    return (0.5 * noise * channel_scale[None] * per_token_scale * head_scale[None]).astype(jnp.bfloat16)


def levels(rng, extent, cuts, low, top_value):
    def one(dim, blocks):
        heights = jax.random.uniform(jax.random.fold_in(jax.random.fold_in(rng, 6), dim), (blocks,), jnp.float32, low / len(cuts), top_value / len(cuts))
        return jnp.repeat(jnp.exp(heights), extent[dim] // blocks).reshape((-1,) + (1,) * (len(extent) - dim - 1))

    loudness = one(*cuts[0])
    for cut in cuts[1:]:
        loudness = loudness * one(*cut)
    return loudness


def gaussian(key, dims, scale, bound, cuts=(), kind=jnp.bfloat16):
    array = scale * jax.random.normal(key, dims, jnp.float32)
    if cuts:
        array = array * levels(key, dims, cuts, -0.22, 0.18)
    return jnp.clip(array, -bound, bound).astype(kind)


def setup_inputs(seed: int = 0) -> dict:
    key_list = jax.random.split(jax.random.key(seed), 8)
    queries = gaussian(key_list[0], (TOKENS, HEADS * DK), 1.0, 6.0, ((0, 8), (1, 4)))
    keys = gaussian(key_list[1], (TOKENS, HEADS * DK), (1.0 / DK), 0.046875, ((0, 8), (1, 4)))
    values = draw_values(jax.random.fold_in(key_list[7], 71), 0)
    out_grad = gaussian(key_list[3], (TOKENS, HEADS * DV), 1.0, 6.0, ((0, 8), (1, 4)))
    log_key_decay = draw_log_key_decay(jax.random.fold_in(key_list[7], 71), 0)
    value_rate = jnp.clip(jnp.exp(math.log(0.05) - 8.317766 * jax.random.uniform(key_list[5], (HEADS * DV,), jnp.float32) ** levels(key_list[5], (HEADS * DV,), ((0, 4),), -0.2, 0.2)), 1.220703143189894e-05, 0.05)
    norm_gain = jnp.clip(1.0 + 0.18 * jax.random.normal(key_list[6], (HEADS * DV,), jnp.float32), 0.1, 1.9)
    return {"queries": queries, "keys": keys, "values": values, "out_grad": out_grad, "log_key_decay": log_key_decay, "value_rate": value_rate, "norm_gain": norm_gain}


highest = lax.Precision.HIGHEST

def prepare(query_block, key_block, value_block, decay_block, value_log):
    key_cumul = jnp.cumsum(decay_block.astype(jnp.float32), axis=0)
    steps_in = (jnp.arange(BL, dtype=jnp.float32) + 1.0)[:, None, None]
    value_cumul = steps_in * value_log[None]
    query_tilde = query_block.astype(jnp.float32) * jnp.exp(key_cumul)
    key_tilde = key_block.astype(jnp.float32) * jnp.exp(-key_cumul)
    value_tilde = value_block.astype(jnp.float32) * jnp.exp(-value_cumul)
    block_decay = jnp.exp(key_cumul[-1])[:, :, None] * jnp.exp(BL * value_log)[:, None, :]
    return (key_cumul, value_cumul, query_tilde, key_tilde, value_tilde, block_decay)

def reference(queries, keys, values, out_grad, log_key_decay, value_rate, norm_gain):
    block_total = TOKENS // BL
    value_log = -value_rate.reshape(HEADS, DV)
    rows_index = jnp.arange(BL)
    causal_mask = (rows_index[:, None] >= rows_index[None, :]).astype(jnp.float32)
    query_blocks = queries.reshape(block_total, BL, HEADS, DK)
    key_blocks = keys.reshape(block_total, BL, HEADS, DK)
    value_blocks = values.reshape(block_total, BL, HEADS, DV)
    decay_blocks = log_key_decay.reshape(block_total, BL, HEADS, DK)
    zero_state = jnp.zeros((HEADS, DK, DV), jnp.float32)

    def forward_block(state, inputs):
        key_cumul, value_cumul, query_tilde, key_tilde, value_tilde, block_decay = prepare(*inputs, value_log)
        scores = jnp.einsum('thi,shi->hts', query_tilde, key_tilde, precision=highest) * causal_mask
        core = jnp.exp(value_cumul) * (jnp.einsum('thi,hij->thj', query_tilde, state, precision=highest) + jnp.einsum('hts,shj->thj', scores, value_tilde, precision=highest))
        kv_sum = jnp.einsum('shi,shj->hij', key_tilde, value_tilde, precision=highest)
        return (block_decay * state + block_decay * kv_sum, core)
    _, core = lax.scan(forward_block, zero_state, (query_blocks, key_blocks, value_blocks, decay_blocks))
    core = core.reshape(TOKENS, HEADS * DV)
    columns = HEADS * DV
    grad_out = out_grad.astype(jnp.float32)
    weighted = grad_out * norm_gain[None]
    rms = lax.rsqrt(lax.optimization_barrier(jnp.sum(core * core, axis=1)) / columns + 1e-06)
    cross = lax.optimization_barrier(jnp.sum(weighted * core, axis=1))
    core_grad = rms[:, None] * weighted - core * (rms * rms * rms * cross / columns)[:, None]
    gain_grad = lax.optimization_barrier(jnp.sum(grad_out * core * rms[:, None], axis=0)) / math.sqrt(TOKENS)
    grad_blocks = core_grad.reshape(block_total, BL, HEADS, DV)

    def query_block_step(state, inputs):
        query_block, key_block, value_block, decay_block, grad_block = inputs
        key_cumul, value_cumul, query_tilde, key_tilde, value_tilde, block_decay = prepare(query_block, key_block, value_block, decay_block, value_log)
        grad_tilde = grad_block * jnp.exp(value_cumul)
        mixed = jnp.einsum('thj,shj->hts', grad_tilde, value_tilde, precision=highest) * causal_mask
        query_part = jnp.exp(key_cumul) * (jnp.einsum('thj,hij->thi', grad_tilde, state, precision=highest) + jnp.einsum('hts,shi->thi', mixed, key_tilde, precision=highest))
        kv_sum = jnp.einsum('shi,shj->hij', key_tilde, value_tilde, precision=highest)
        return (block_decay * state + block_decay * kv_sum, query_part.astype(jnp.bfloat16))
    _, query_grad = lax.scan(query_block_step, zero_state, (query_blocks, key_blocks, value_blocks, decay_blocks, grad_blocks))

    def adjoint_block(carry, inputs):
        query_block, key_block, value_block, decay_block, grad_block = inputs
        key_cumul, value_cumul, query_tilde, key_tilde, value_tilde, block_decay = prepare(query_block, key_block, value_block, decay_block, value_log)
        grad_tilde = grad_block * jnp.exp(value_cumul)
        mixed = jnp.einsum('thj,shj->hts', grad_tilde, value_tilde, precision=highest) * causal_mask
        scores = jnp.einsum('thi,shi->hts', query_tilde, key_tilde, precision=highest) * causal_mask
        passed = block_decay * carry
        key_part = jnp.exp(-key_cumul) * (jnp.einsum('hts,thi->shi', mixed, query_tilde, precision=highest) + jnp.einsum('shj,hij->shi', value_tilde, passed, precision=highest))
        value_part = jnp.exp(-value_cumul) * (jnp.einsum('hts,thj->shj', scores, grad_tilde, precision=highest) + jnp.einsum('shi,hij->shj', key_tilde, passed, precision=highest))
        new_carry = jnp.einsum('thi,thj->hij', query_tilde, grad_tilde, precision=highest) + passed
        return (new_carry, (key_part.astype(jnp.bfloat16), value_part.astype(jnp.bfloat16)))
    _, (key_grad, value_grad) = lax.scan(adjoint_block, zero_state, (query_blocks, key_blocks, value_blocks, decay_blocks, grad_blocks), reverse=True)
    return (query_grad.reshape(TOKENS, HEADS * DK), key_grad.reshape(TOKENS, HEADS * DK), value_grad.reshape(TOKENS, HEADS * DV), gain_grad)
```

```python
import functools
import math

import jax
import jax.numpy as jnp
from jax import lax
from jax.experimental import pallas as pl
from jax.experimental.pallas import tpu as pltpu
from jax.sharding import PartitionSpec as P

D = 128
BL = 128
MESH = pl.DeviceIdType.MESH
f32 = jnp.float32
bf16 = jnp.bfloat16


def split(x):
    high = x.astype(bf16)
    return high, (x - high.astype(f32)).astype(bf16)


def product(pairs, left_dim, right_dim):
    def dot(left, right):
        return lax.dot_general(
            left, right, (((left_dim,), (right_dim,)), ((), ())), preferred_element_type=f32
        )

    total = None
    for (ah, al), (bh, bl) in pairs:
        part = dot(ah, bh) + (dot(ah, bl) + dot(al, bh))
        total = part if total is None else total + part
    return total


def nn(*pairs):
    return product(pairs, 1, 0)


def nt(*pairs):
    return product(pairs, 1, 1)


def tn(*pairs):
    return product(pairs, 0, 0)


def kernel(
    sizes,
    q_ref, k_ref, v_ref, og_ref, decay_ref, rate_ref, gain_ref,
    qg_ref, kg_ref, vg_ref, gg_ref,
    c_ref, qh_ref, ql_ref, kh_ref, kl_ref, gh_ref, gl_ref,
    core_ref, sc_ref, start_ref, end_ref,
    last_ref, total_ref, local_ref,
    fr_ref, fs_ref, ar_ref, as_ref,
    sq_ref, cr_ref, hs_ref, gs_ref,
    fr_sem, fs_sem, ar_sem, as_sem, hr_sem, hs_sem, gr_sem, gs_sem,
):
    n_outer, n_inner, n_head = sizes
    n = n_outer * n_inner
    rows_all, cols_all = q_ref.shape
    heads = cols_all // D
    blocks = rows_all // BL
    p = lax.axis_index("outer") * n_inner + lax.axis_index("inner")
    me = lax.axis_index("head")

    def seq_device(i):
        return {"outer": i // n_inner, "inner": lax.rem(i, n_inner)}

    barrier = pltpu.get_barrier_semaphore()

    def greet_seq(i, _):
        pl.semaphore_signal(
            barrier, inc=1, device_id=seq_device(lax.rem(p + i, n)), device_id_type=MESH
        )
        return 0

    lax.fori_loop(1, n, greet_seq, 0)
    for i in range(1, n_head):
        pl.semaphore_signal(
            barrier, inc=1, device_id={"head": lax.rem(me + i, n_head)}, device_id_type=MESH
        )

    row_id = lax.broadcasted_iota(jnp.int32, (BL, BL), 0)
    col_id = lax.broadcasted_iota(jnp.int32, (BL, BL), 1)
    causal = row_id >= col_id
    steps_in = (lax.broadcasted_iota(jnp.int32, (BL, D), 0) + 1).astype(f32)
    span = float(BL)

    def rows(b):
        return pl.ds(pl.multiple_of(b * BL, BL), BL)

    def cols(h):
        return pl.ds(pl.multiple_of(h * D, D), D)

    def rate_row(h):
        return rate_ref[pl.ds(h, 1), :]

    def rate_down(h):
        return jnp.broadcast_to(rate_row(h), (D, D)).T

    def last_row(h, b):
        return last_ref[pl.ds(h * blocks + b, 1), :]

    def pieces(high, low, b, h):
        return high[rows(b), cols(h)], low[rows(b), cols(h)]

    def value_tilde(b, h, shrink):
        return split(v_ref[rows(b), cols(h)].astype(f32) * shrink)

    def prepare(h, _):
        down = rate_down(h)
        shrink = jnp.exp(steps_in * rate_row(h))
        ones = causal.astype(bf16)

        def block(b, carry):
            state, key_sum = carry
            d = decay_ref[rows(b), cols(h)]
            d1 = d.astype(bf16)
            rest = d - d1.astype(f32)
            d2 = rest.astype(bf16)
            d3 = (rest - d2.astype(f32)).astype(bf16)
            sums = jnp.dot(
                ones, jnp.concatenate([d1, d2, d3], axis=1), preferred_element_type=f32
            )
            c = sums[:, :D] + (sums[:, D : 2 * D] + sums[:, 2 * D :])
            c_ref[rows(b), cols(h)] = c
            last = c[BL - 1 :, :]
            last_ref[pl.ds(h * blocks + b, 1), :] = last
            kt = split(k_ref[rows(b), cols(h)].astype(f32) * jnp.exp(-c))
            qt = split(q_ref[rows(b), cols(h)].astype(f32) * jnp.exp(c))
            kh_ref[rows(b), cols(h)], kl_ref[rows(b), cols(h)] = kt
            qh_ref[rows(b), cols(h)], ql_ref[rows(b), cols(h)] = qt
            kv = tn((value_tilde(b, h, shrink), kt))
            start_ref[h * blocks + b] = state
            return jnp.exp(last - span * down) * (state + kv), key_sum + last

        state, key_sum = lax.fori_loop(
            0, blocks, block, (jnp.zeros((D, D), f32), jnp.zeros((1, D), f32)), unroll=UNROLL
        )
        local_ref[h] = state
        total_ref[pl.ds(h, 1), :] = key_sum
        return 0

    lax.fori_loop(0, heads, prepare, 0)
    pl.semaphore_wait(barrier, n - 1 + n_head - 1)

    def device_decay(h):
        return jnp.exp(total_ref[pl.ds(h, 1), :] - float(rows_all) * rate_down(h))

    def chain(h, first, last, device, recv, send, recv_sem, send_sem):
        copy = pltpu.make_async_remote_copy(
            src_ref=send.at[h],
            dst_ref=recv.at[h],
            send_sem=send_sem.at[h],
            recv_sem=recv_sem.at[h],
            device_id=device,
            device_id_type=MESH,
        )

        @pl.when(p != first)
        def _():
            copy.wait_recv()

        @pl.when(p != last)
        def _():
            send[h] = device_decay(h) * recv[h] + local_ref[h]
            copy.start()

    def drain(h, last, device, recv, send, recv_sem, send_sem):
        copy = pltpu.make_async_remote_copy(
            src_ref=send.at[h],
            dst_ref=recv.at[h],
            send_sem=send_sem.at[h],
            recv_sem=recv_sem.at[h],
            device_id=device,
            device_id_type=MESH,
        )

        @pl.when(p != last)
        def _():
            copy.wait_send()

    def inside(h, _):
        shrink = jnp.exp(steps_in * rate_row(h))

        def block(b, _):
            qt = pieces(qh_ref, ql_ref, b, h)
            kt = pieces(kh_ref, kl_ref, b, h)
            scores = jnp.where(causal, nt((qt, kt)), 0.0)
            sc_ref[rows(b), cols(h)] = scores
            core_ref[rows(b), cols(h)] = nn((split(scores), value_tilde(b, h, shrink)))
            return 0

        lax.fori_loop(0, blocks, block, 0, unroll=UNROLL)
        return 0

    right = seq_device(lax.rem(p + 1, n))
    left = seq_device(lax.rem(p + n - 1, n))

    @pl.when(p == 0)
    def _():
        fr_ref[...] = jnp.zeros_like(fr_ref)

    @pl.when(p == n - 1)
    def _():
        ar_ref[...] = jnp.zeros_like(ar_ref)

    ahead = jnp.minimum(heads, 3 * p)
    lax.fori_loop(0, ahead, inside, 0)

    def forward_chain(h, _):
        chain(h, 0, n - 1, right, fr_ref, fs_ref, fr_sem, fs_sem)
        return 0

    lax.fori_loop(0, heads, forward_chain, 0)
    lax.fori_loop(ahead, heads, inside, 0)

    sq_ref[...] = jnp.zeros_like(sq_ref)
    cr_ref[...] = jnp.zeros_like(cr_ref)

    def finish_core(h, _):
        down = rate_down(h)
        growth = jnp.exp(-steps_in * rate_row(h))
        gain = gain_ref[pl.ds(h, 1), :]

        def block(b, before):
            decay = jnp.exp(before - (b * BL).astype(f32) * down)
            state = start_ref[h * blocks + b] + decay * fr_ref[h]
            start_ref[h * blocks + b] = state
            core = growth * (
                core_ref[rows(b), cols(h)]
                + nt((pieces(qh_ref, ql_ref, b, h), split(state)))
            )
            core_ref[rows(b), cols(h)] = core
            weighted = og_ref[rows(b), cols(h)].astype(f32) * gain
            sq_ref[rows(b), :] += core * core
            cr_ref[rows(b), :] += weighted * core
            return before + last_row(h, b)

        lax.fori_loop(0, blocks, block, jnp.zeros((1, D), f32), unroll=UNROLL)
        return 0

    lax.fori_loop(0, heads, finish_core, 0)

    for b in range(blocks):
        for ref, place in ((sq_ref, b), (cr_ref, blocks + b)):
            across = ref[b * BL : (b + 1) * BL, :].T
            hs_ref[me, pl.ds(place, 1), :] = jnp.sum(across, axis=0, keepdims=True)

    def head_copy(i):
        peer = lax.rem(me + i, n_head)
        return pltpu.make_async_remote_copy(
            src_ref=hs_ref.at[me],
            dst_ref=hs_ref.at[me],
            send_sem=hs_sem.at[i - 1],
            recv_sem=hr_sem.at[i - 1],
            device_id={"head": peer},
            device_id_type=MESH,
        )

    for i in range(1, n_head):
        head_copy(i).start()
    for i in range(1, n_head):
        head_copy(i).wait_recv()
    sums = hs_ref[0]
    for i in range(1, n_head):
        sums = sums + hs_ref[i]
    columns = float(cols_all * n_head)
    inverse = lax.rsqrt(sums[:blocks] / columns + 1e-06)
    slope = inverse * inverse * inverse * sums[blocks:] / columns
    for b in range(blocks):
        for ref, value in ((sq_ref, inverse), (cr_ref, slope)):
            ref[b * BL : (b + 1) * BL, :] = jnp.broadcast_to(value[b : b + 1], (BL, BL)).T

    def start_adjoint(h, _):
        down = rate_down(h)
        growth = jnp.exp(-steps_in * rate_row(h))
        gain = gain_ref[pl.ds(h, 1), :]

        def block(step, carry):
            adjoint, gain_sum = carry
            b = blocks - 1 - step
            grad_out = og_ref[rows(b), cols(h)].astype(f32)
            core = core_ref[rows(b), cols(h)]
            normed = grad_out * sq_ref[rows(b), :]
            gain_sum = gain_sum + jnp.sum(normed * core, axis=0, keepdims=True)
            gt = split((normed * gain - core * cr_ref[rows(b), :]) * growth)
            gh_ref[rows(b), cols(h)], gl_ref[rows(b), cols(h)] = gt
            end_ref[h * blocks + b] = adjoint
            addend = tn((gt, pieces(qh_ref, ql_ref, b, h)))
            return addend + jnp.exp(last_row(h, b) - span * down) * adjoint, gain_sum

        adjoint, gain_sum = lax.fori_loop(
            0, blocks, block, (jnp.zeros((D, D), f32), jnp.zeros((1, D), f32)), unroll=UNROLL
        )
        local_ref[h] = adjoint
        gs_ref[p, pl.ds(h, 1), :] = gain_sum
        return 0

    lax.fori_loop(0, heads, start_adjoint, 0)

    def middle(h, _):
        shrink = jnp.exp(steps_in * rate_row(h))

        def block(b, _):
            gt = pieces(gh_ref, gl_ref, b, h)
            qt = pieces(qh_ref, ql_ref, b, h)
            kt = pieces(kh_ref, kl_ref, b, h)
            mixed = split(jnp.where(causal, nt((gt, value_tilde(b, h, shrink))), 0.0))
            state = split(start_ref[h * blocks + b])
            scores = split(sc_ref[rows(b), cols(h)])
            query_part = jnp.exp(c_ref[rows(b), cols(h)]) * nn((gt, state), (mixed, kt))
            qg_ref[rows(b), cols(h)] = query_part.astype(bf16)
            core_ref[rows(b), cols(h)] = tn((mixed, qt))
            sc_ref[rows(b), cols(h)] = tn((scores, gt))
            return 0

        lax.fori_loop(0, blocks, block, 0, unroll=UNROLL)
        return 0

    def gain_copy(i):
        return pltpu.make_async_remote_copy(
            src_ref=gs_ref.at[p],
            dst_ref=gs_ref.at[p],
            send_sem=gs_sem.at[i - 1],
            recv_sem=gr_sem.at[i - 1],
            device_id=seq_device(lax.rem(p + i, n)),
            device_id_type=MESH,
        )

    ahead = jnp.minimum(heads, n - 1 - p)
    lax.fori_loop(0, ahead, middle, 0)

    def backward_chain(h, _):
        chain(h, n - 1, 0, left, ar_ref, as_ref, ar_sem, as_sem)
        return 0

    lax.fori_loop(0, heads, backward_chain, 0)

    def gain_start(i, _):
        gain_copy(i).start()
        return 0

    lax.fori_loop(1, n, gain_start, 0)
    lax.fori_loop(ahead, heads, middle, 0)

    def finish(h, _):
        down = rate_down(h)
        shrink = jnp.exp(steps_in * rate_row(h))

        def block(step, after):
            b = blocks - 1 - step
            last = last_row(h, b)
            decay = jnp.exp(after - (step * BL).astype(f32) * down)
            end = end_ref[h * blocks + b] + decay * ar_ref[h]
            passed = split(jnp.exp(last - span * down) * end)
            kt = pieces(kh_ref, kl_ref, b, h)
            key_part = jnp.exp(-c_ref[rows(b), cols(h)]) * (
                core_ref[rows(b), cols(h)] + nn((value_tilde(b, h, shrink), passed))
            )
            kg_ref[rows(b), cols(h)] = key_part.astype(bf16)
            value_part = shrink * (sc_ref[rows(b), cols(h)] + nt((kt, passed)))
            vg_ref[rows(b), cols(h)] = value_part.astype(bf16)
            return after + last

        lax.fori_loop(0, blocks, block, jnp.zeros((1, D), f32), unroll=UNROLL)
        return 0

    lax.fori_loop(0, heads, finish, 0)

    def gain_wait(i, _):
        gain_copy(i).wait_recv()
        return 0

    lax.fori_loop(1, n, gain_wait, 0)

    def gain_add(i, total):
        return total + gs_ref[i]

    total = lax.fori_loop(1, n, gain_add, gs_ref[0])
    gg_ref[...] = total / math.sqrt(rows_all * n)

    def drain_all(h, _):
        drain(h, n - 1, right, fr_ref, fs_ref, fr_sem, fs_sem)
        drain(h, 0, left, ar_ref, as_ref, ar_sem, as_sem)
        return 0

    lax.fori_loop(0, heads, drain_all, 0)
    for i in range(1, n_head):
        head_copy(i).wait_send()

    def gain_drain(i, _):
        gain_copy(i).wait_send()
        return 0

    lax.fori_loop(1, n, gain_drain, 0)


UNROLL = 2


def on_device(sizes, queries, keys, values, out_grad, log_key_decay, value_rate, norm_gain):
    t, c = queries.shape
    heads, blocks = c // D, t // BL
    n = sizes[0] * sizes[1]
    n_head = sizes[2]
    vmem = pl.BlockSpec(memory_space=pltpu.VMEM)
    whole = lambda dtype: pltpu.VMEM((t, c), dtype)
    states = lambda count: pltpu.VMEM((count, D, D), f32)
    dma = lambda count: pltpu.SemaphoreType.DMA((count,))
    out = pl.pallas_call(
        functools.partial(kernel, sizes),
        out_shape=[jax.ShapeDtypeStruct((t, c), bf16)] * 3
        + [jax.ShapeDtypeStruct((heads, D), f32)],
        in_specs=[vmem] * 7,
        out_specs=[vmem] * 4,
        scratch_shapes=[
            whole(f32), whole(bf16), whole(bf16), whole(bf16), whole(bf16), whole(bf16),
            whole(bf16), whole(f32), whole(f32), states(heads * blocks), states(heads * blocks),
            pltpu.VMEM((heads * blocks, D), f32), pltpu.VMEM((heads, D), f32), states(heads),
            states(heads), states(heads), states(heads), states(heads),
            pltpu.VMEM((t, D), f32), pltpu.VMEM((t, D), f32),
            pltpu.VMEM((n_head, 2 * blocks, D), f32), pltpu.VMEM((n, heads, D), f32),
            dma(heads), dma(heads), dma(heads), dma(heads),
            dma(max(n_head - 1, 1)), dma(max(n_head - 1, 1)),
            dma(max(n - 1, 1)), dma(max(n - 1, 1)),
        ],
        compiler_params=pltpu.CompilerParams(
            collective_id=0, has_side_effects=True, vmem_limit_bytes=63 * 1024 * 1024
        ),
        name="recurrence_backward",
    )(
        queries,
        keys,
        values,
        out_grad,
        log_key_decay,
        value_rate.reshape(heads, D),
        norm_gain.reshape(heads, D),
    )
    return out[0], out[1], out[2], out[3].reshape(c)


def solution(mesh):
    split_all = P(("outer", "inner"), "head")
    sizes = tuple(mesh.shape[name] for name in ("outer", "inner", "head"))
    return jax.shard_map(
        functools.partial(on_device, sizes),
        mesh=mesh,
        in_specs=(split_all,) * 5 + (P("head"), P("head")),
        out_specs=(split_all,) * 3 + (P("head"),),
        check_vma=False,
    )
```

```python
import functools
import math

import jax
import jax.numpy as jnp
from jax import lax
from jax.experimental import pallas as pl
from jax.experimental.pallas import tpu as pltpu
from jax.sharding import PartitionSpec as P

D = 128
BL = 128
MESH = pl.DeviceIdType.MESH
f32 = jnp.float32
bf16 = jnp.bfloat16


def split(x):
    high = x.astype(bf16)
    return high, (x - high.astype(f32)).astype(bf16)


def product(pairs, left_dim, right_dim):
    def dot(left, right):
        return lax.dot_general(
            left, right, (((left_dim,), (right_dim,)), ((), ())), preferred_element_type=f32
        )

    total = None
    for (ah, al), (bh, bl) in pairs:
        both = dot(ah, jnp.concatenate([bh, bl], axis=1 - right_dim))
        part = both[:, :D] + (both[:, D:] + dot(al, bh))
        total = part if total is None else total + part
    return total


def nn(*pairs):
    return product(pairs, 1, 0)


def nt(*pairs):
    return product(pairs, 1, 1)


def tn(*pairs):
    return product(pairs, 0, 0)


def kernel(
    sizes,
    q_ref, k_ref, v_ref, og_ref, decay_ref, rate_ref, gain_ref,
    qg_ref, kg_ref, vg_ref, gg_ref,
    c_ref, qh_ref, ql_ref, kh_ref, kl_ref, gh_ref, gl_ref,
    core_ref, sc_ref, start_ref, end_ref,
    last_ref, total_ref, local_ref,
    fr_ref, fs_ref, ar_ref, as_ref,
    sq_ref, cr_ref, hs_ref, gs_ref,
    fr_sem, fs_sem, ar_sem, as_sem, hr_sem, hs_sem, gr_sem, gs_sem,
):
    n_outer, n_inner, n_head = sizes
    n = n_outer * n_inner
    rows_all, cols_all = q_ref.shape
    heads = cols_all // D
    blocks = rows_all // BL
    p = lax.axis_index("outer") * n_inner + lax.axis_index("inner")
    me = lax.axis_index("head")

    def seq_device(i):
        return {"outer": i // n_inner, "inner": lax.rem(i, n_inner)}

    barrier = pltpu.get_barrier_semaphore()

    def greet_seq(i, _):
        pl.semaphore_signal(
            barrier, inc=1, device_id=seq_device(lax.rem(p + i, n)), device_id_type=MESH
        )
        return 0

    lax.fori_loop(1, n, greet_seq, 0)
    for i in range(1, n_head):
        pl.semaphore_signal(
            barrier, inc=1, device_id={"head": lax.rem(me + i, n_head)}, device_id_type=MESH
        )

    row_id = lax.broadcasted_iota(jnp.int32, (BL, BL), 0)
    col_id = lax.broadcasted_iota(jnp.int32, (BL, BL), 1)
    causal = row_id >= col_id
    steps_in = (lax.broadcasted_iota(jnp.int32, (BL, D), 0) + 1).astype(f32)
    span = float(BL)

    def rows(b):
        return pl.ds(pl.multiple_of(b * BL, BL), BL)

    def cols(h):
        return pl.ds(pl.multiple_of(h * D, D), D)

    def rate_row(h):
        return rate_ref[pl.ds(h, 1), :]

    def rate_down(h):
        return jnp.broadcast_to(rate_row(h), (D, D)).T

    def last_row(h, b):
        return last_ref[pl.ds(h * blocks + b, 1), :]

    def pieces(high, low, b, h):
        return high[rows(b), cols(h)], low[rows(b), cols(h)]

    def value_tilde(b, h, shrink):
        return split(v_ref[rows(b), cols(h)].astype(f32) * shrink)

    def prepare(h, _):
        down = rate_down(h)
        shrink = jnp.exp(steps_in * rate_row(h))
        ones = causal.astype(bf16)

        def block(b, carry):
            state, key_sum = carry
            d = decay_ref[rows(b), cols(h)]
            d1 = d.astype(bf16)
            rest = d - d1.astype(f32)
            d2 = rest.astype(bf16)
            d3 = (rest - d2.astype(f32)).astype(bf16)
            sums = jnp.dot(
                ones, jnp.concatenate([d1, d2, d3], axis=1), preferred_element_type=f32
            )
            c = sums[:, :D] + (sums[:, D : 2 * D] + sums[:, 2 * D :])
            c_ref[rows(b), cols(h)] = c
            last = c[BL - 1 :, :]
            last_ref[pl.ds(h * blocks + b, 1), :] = last
            kt = split(k_ref[rows(b), cols(h)].astype(f32) * jnp.exp(-c))
            qt = split(q_ref[rows(b), cols(h)].astype(f32) * jnp.exp(c))
            kh_ref[rows(b), cols(h)], kl_ref[rows(b), cols(h)] = kt
            qh_ref[rows(b), cols(h)], ql_ref[rows(b), cols(h)] = qt
            kv = tn((value_tilde(b, h, shrink), kt))
            start_ref[h * blocks + b] = state
            return jnp.exp(last - span * down) * (state + kv), key_sum + last

        state, key_sum = lax.fori_loop(
            0, blocks, block, (jnp.zeros((D, D), f32), jnp.zeros((1, D), f32)), unroll=UNROLL
        )
        local_ref[h] = state
        total_ref[pl.ds(h, 1), :] = key_sum
        return 0

    lax.fori_loop(0, heads, prepare, 0)
    pl.semaphore_wait(barrier, n - 1 + n_head - 1)

    def device_decay(h):
        return jnp.exp(total_ref[pl.ds(h, 1), :] - float(rows_all) * rate_down(h))

    def chain(h, first, last, device, recv, send, recv_sem, send_sem):
        copy = pltpu.make_async_remote_copy(
            src_ref=send.at[h],
            dst_ref=recv.at[h],
            send_sem=send_sem.at[h],
            recv_sem=recv_sem.at[h],
            device_id=device,
            device_id_type=MESH,
        )

        @pl.when(p != first)
        def _():
            copy.wait_recv()

        @pl.when(p != last)
        def _():
            send[h] = device_decay(h) * recv[h] + local_ref[h]
            copy.start()

    def drain(h, last, device, recv, send, recv_sem, send_sem):
        copy = pltpu.make_async_remote_copy(
            src_ref=send.at[h],
            dst_ref=recv.at[h],
            send_sem=send_sem.at[h],
            recv_sem=recv_sem.at[h],
            device_id=device,
            device_id_type=MESH,
        )

        @pl.when(p != last)
        def _():
            copy.wait_send()

    def inside(h, _):
        shrink = jnp.exp(steps_in * rate_row(h))

        def block(b, _):
            qt = pieces(qh_ref, ql_ref, b, h)
            kt = pieces(kh_ref, kl_ref, b, h)
            scores = jnp.where(causal, nt((qt, kt)), 0.0)
            sc_ref[rows(b), cols(h)] = scores
            core_ref[rows(b), cols(h)] = nn((split(scores), value_tilde(b, h, shrink)))
            return 0

        lax.fori_loop(0, blocks, block, 0, unroll=UNROLL)
        return 0

    right = seq_device(lax.rem(p + 1, n))
    left = seq_device(lax.rem(p + n - 1, n))

    @pl.when(p == 0)
    def _():
        fr_ref[...] = jnp.zeros_like(fr_ref)

    @pl.when(p == n - 1)
    def _():
        ar_ref[...] = jnp.zeros_like(ar_ref)

    ahead = jnp.minimum(heads, 3 * p)
    lax.fori_loop(0, ahead, inside, 0)

    def forward_chain(h, _):
        chain(h, 0, n - 1, right, fr_ref, fs_ref, fr_sem, fs_sem)
        return 0

    lax.fori_loop(0, heads, forward_chain, 0)
    lax.fori_loop(ahead, heads, inside, 0)

    sq_ref[...] = jnp.zeros_like(sq_ref)
    cr_ref[...] = jnp.zeros_like(cr_ref)

    def finish_core(h, _):
        down = rate_down(h)
        growth = jnp.exp(-steps_in * rate_row(h))
        gain = gain_ref[pl.ds(h, 1), :]

        def block(b, before):
            decay = jnp.exp(before - (b * BL).astype(f32) * down)
            state = start_ref[h * blocks + b] + decay * fr_ref[h]
            start_ref[h * blocks + b] = state
            core = growth * (
                core_ref[rows(b), cols(h)]
                + nt((pieces(qh_ref, ql_ref, b, h), split(state)))
            )
            core_ref[rows(b), cols(h)] = core
            weighted = og_ref[rows(b), cols(h)].astype(f32) * gain
            sq_ref[rows(b), :] += core * core
            cr_ref[rows(b), :] += weighted * core
            return before + last_row(h, b)

        lax.fori_loop(0, blocks, block, jnp.zeros((1, D), f32), unroll=UNROLL)
        return 0

    lax.fori_loop(0, heads, finish_core, 0)

    for b in range(blocks):
        for ref, place in ((sq_ref, b), (cr_ref, blocks + b)):
            across = ref[b * BL : (b + 1) * BL, :].T
            hs_ref[me, pl.ds(place, 1), :] = jnp.sum(across, axis=0, keepdims=True)

    def head_copy(i):
        peer = lax.rem(me + i, n_head)
        return pltpu.make_async_remote_copy(
            src_ref=hs_ref.at[me],
            dst_ref=hs_ref.at[me],
            send_sem=hs_sem.at[i - 1],
            recv_sem=hr_sem.at[i - 1],
            device_id={"head": peer},
            device_id_type=MESH,
        )

    for i in range(1, n_head):
        head_copy(i).start()
    for i in range(1, n_head):
        head_copy(i).wait_recv()
    sums = hs_ref[0]
    for i in range(1, n_head):
        sums = sums + hs_ref[i]
    columns = float(cols_all * n_head)
    inverse = lax.rsqrt(sums[:blocks] / columns + 1e-06)
    slope = inverse * inverse * inverse * sums[blocks:] / columns
    for b in range(blocks):
        for ref, value in ((sq_ref, inverse), (cr_ref, slope)):
            ref[b * BL : (b + 1) * BL, :] = jnp.broadcast_to(value[b : b + 1], (BL, BL)).T

    def start_adjoint(h, _):
        down = rate_down(h)
        growth = jnp.exp(-steps_in * rate_row(h))
        gain = gain_ref[pl.ds(h, 1), :]

        def block(step, carry):
            adjoint, gain_sum = carry
            b = blocks - 1 - step
            grad_out = og_ref[rows(b), cols(h)].astype(f32)
            core = core_ref[rows(b), cols(h)]
            normed = grad_out * sq_ref[rows(b), :]
            gain_sum = gain_sum + jnp.sum(normed * core, axis=0, keepdims=True)
            gt = split((normed * gain - core * cr_ref[rows(b), :]) * growth)
            gh_ref[rows(b), cols(h)], gl_ref[rows(b), cols(h)] = gt
            end_ref[h * blocks + b] = adjoint
            addend = tn((gt, pieces(qh_ref, ql_ref, b, h)))
            return addend + jnp.exp(last_row(h, b) - span * down) * adjoint, gain_sum

        adjoint, gain_sum = lax.fori_loop(
            0, blocks, block, (jnp.zeros((D, D), f32), jnp.zeros((1, D), f32)), unroll=UNROLL
        )
        local_ref[h] = adjoint
        gs_ref[p, pl.ds(h, 1), :] = gain_sum
        return 0

    lax.fori_loop(0, heads, start_adjoint, 0)

    def middle(h, _):
        shrink = jnp.exp(steps_in * rate_row(h))

        def block(b, _):
            gt = pieces(gh_ref, gl_ref, b, h)
            qt = pieces(qh_ref, ql_ref, b, h)
            kt = pieces(kh_ref, kl_ref, b, h)
            mixed = split(jnp.where(causal, nt((gt, value_tilde(b, h, shrink))), 0.0))
            state = split(start_ref[h * blocks + b])
            scores = split(sc_ref[rows(b), cols(h)])
            query_part = jnp.exp(c_ref[rows(b), cols(h)]) * nn((gt, state), (mixed, kt))
            qg_ref[rows(b), cols(h)] = query_part.astype(bf16)
            core_ref[rows(b), cols(h)] = tn((mixed, qt))
            sc_ref[rows(b), cols(h)] = tn((scores, gt))
            return 0

        lax.fori_loop(0, blocks, block, 0, unroll=UNROLL)
        return 0

    def gain_copy(i):
        return pltpu.make_async_remote_copy(
            src_ref=gs_ref.at[p],
            dst_ref=gs_ref.at[p],
            send_sem=gs_sem.at[i - 1],
            recv_sem=gr_sem.at[i - 1],
            device_id=seq_device(lax.rem(p + i, n)),
            device_id_type=MESH,
        )

    ahead = jnp.minimum(heads, n - 1 - p)
    lax.fori_loop(0, ahead, middle, 0)

    def backward_chain(h, _):
        chain(h, n - 1, 0, left, ar_ref, as_ref, ar_sem, as_sem)
        return 0

    lax.fori_loop(0, heads, backward_chain, 0)

    def gain_start(i, _):
        gain_copy(i).start()
        return 0

    lax.fori_loop(1, n, gain_start, 0)
    lax.fori_loop(ahead, heads, middle, 0)

    def finish(h, _):
        down = rate_down(h)
        shrink = jnp.exp(steps_in * rate_row(h))

        def block(step, after):
            b = blocks - 1 - step
            last = last_row(h, b)
            decay = jnp.exp(after - (step * BL).astype(f32) * down)
            end = end_ref[h * blocks + b] + decay * ar_ref[h]
            passed = split(jnp.exp(last - span * down) * end)
            kt = pieces(kh_ref, kl_ref, b, h)
            key_part = jnp.exp(-c_ref[rows(b), cols(h)]) * (
                core_ref[rows(b), cols(h)] + nn((value_tilde(b, h, shrink), passed))
            )
            kg_ref[rows(b), cols(h)] = key_part.astype(bf16)
            value_part = shrink * (sc_ref[rows(b), cols(h)] + nt((kt, passed)))
            vg_ref[rows(b), cols(h)] = value_part.astype(bf16)
            return after + last

        lax.fori_loop(0, blocks, block, jnp.zeros((1, D), f32), unroll=UNROLL)
        return 0

    lax.fori_loop(0, heads, finish, 0)

    def gain_wait(i, _):
        gain_copy(i).wait_recv()
        return 0

    lax.fori_loop(1, n, gain_wait, 0)

    def gain_add(i, total):
        return total + gs_ref[i]

    total = lax.fori_loop(1, n, gain_add, gs_ref[0])
    gg_ref[...] = total / math.sqrt(rows_all * n)

    def drain_all(h, _):
        drain(h, n - 1, right, fr_ref, fs_ref, fr_sem, fs_sem)
        drain(h, 0, left, ar_ref, as_ref, ar_sem, as_sem)
        return 0

    lax.fori_loop(0, heads, drain_all, 0)
    for i in range(1, n_head):
        head_copy(i).wait_send()

    def gain_drain(i, _):
        gain_copy(i).wait_send()
        return 0

    lax.fori_loop(1, n, gain_drain, 0)


UNROLL = 4


def on_device(sizes, queries, keys, values, out_grad, log_key_decay, value_rate, norm_gain):
    t, c = queries.shape
    heads, blocks = c // D, t // BL
    n = sizes[0] * sizes[1]
    n_head = sizes[2]
    vmem = pl.BlockSpec(memory_space=pltpu.VMEM)
    whole = lambda dtype: pltpu.VMEM((t, c), dtype)
    states = lambda count: pltpu.VMEM((count, D, D), f32)
    dma = lambda count: pltpu.SemaphoreType.DMA((count,))
    out = pl.pallas_call(
        functools.partial(kernel, sizes),
        out_shape=[jax.ShapeDtypeStruct((t, c), bf16)] * 3
        + [jax.ShapeDtypeStruct((heads, D), f32)],
        in_specs=[vmem] * 7,
        out_specs=[vmem] * 4,
        scratch_shapes=[
            whole(f32), whole(bf16), whole(bf16), whole(bf16), whole(bf16), whole(bf16),
            whole(bf16), whole(f32), whole(f32), states(heads * blocks), states(heads * blocks),
            pltpu.VMEM((heads * blocks, D), f32), pltpu.VMEM((heads, D), f32), states(heads),
            states(heads), states(heads), states(heads), states(heads),
            pltpu.VMEM((t, D), f32), pltpu.VMEM((t, D), f32),
            pltpu.VMEM((n_head, 2 * blocks, D), f32), pltpu.VMEM((n, heads, D), f32),
            dma(heads), dma(heads), dma(heads), dma(heads),
            dma(max(n_head - 1, 1)), dma(max(n_head - 1, 1)),
            dma(max(n - 1, 1)), dma(max(n - 1, 1)),
        ],
        compiler_params=pltpu.CompilerParams(
            collective_id=0, has_side_effects=True, vmem_limit_bytes=63 * 1024 * 1024
        ),
        name="recurrence_backward",
    )(
        queries,
        keys,
        values,
        out_grad,
        log_key_decay,
        value_rate.reshape(heads, D),
        norm_gain.reshape(heads, D),
    )
    return out[0], out[1], out[2], out[3].reshape(c)


def solution(mesh):
    split_all = P(("outer", "inner"), "head")
    sizes = tuple(mesh.shape[name] for name in ("outer", "inner", "head"))
    return jax.shard_map(
        functools.partial(on_device, sizes),
        mesh=mesh,
        in_specs=(split_all,) * 5 + (P("head"), P("head")),
        out_specs=(split_all,) * 3 + (P("head"),),
        check_vma=False,
    )
```
